32 devices in a mesh: groups: 2 (over y), lat: 16 (over z, x, core).
Axes of the slice: x: 2, y: 2, z: 4, core: 2. Of those that a mesh axis runs over, the one named last changes fastest.
Arguments:
- grid_state: bfloat16 [8192, 227], P(('groups', 'lat')), parts along dimension 0, may hold values from -6 to 6
- mesh_embed: bfloat16 [1024, 512], P(('groups', 'lat')), parts along dimension 0, may hold values from -6 to 6
- g2m_owner: int32 [8192, 2], P(('groups', 'lat')), parts along dimension 0, may hold values from 0 to 15, all different within a row; in each aligned block of 256 rows (0 to 255, 256 to 511, ...) at most 64 rows name the same one
- g2m_node: int32 [8192, 2], P(('groups', 'lat')), parts along dimension 0, may hold values from 0 to 31
- mm_owner: int32 [1024, 8], P(('groups', 'lat')), parts along dimension 0, may hold values from 0 to 15, all different within a row; in each aligned block of 32 rows (0 to 31, 32 to 63, ...) at most 32 rows name the same one
- mm_node: int32 [1024, 8], P(('groups', 'lat')), parts along dimension 0, may hold values from 0 to 31
- m2g_owner: int32 [8192, 3], P(('groups', 'lat')), parts along dimension 0, may hold values from 0 to 15, all different within a row; in each aligned block of 256 rows (0 to 255, 256 to 511, ...) at most 96 rows name the same one
- m2g_node: int32 [8192, 3], P(('groups', 'lat')), parts along dimension 0, may hold values from 0 to 31
- embed_in: bfloat16 [227, 512], replicated, may hold values from -0.375 to 0.375
- embed_out: bfloat16 [512, 512], replicated, may hold values from -0.25 to 0.25
- g2m_in: bfloat16 [1024, 512], replicated, may hold values from -0.1875 to 0.1875
- g2m_out: bfloat16 [512, 512], replicated, may hold values from -0.25 to 0.25
- mesh_in: bfloat16 [1024, 512], replicated, may hold values from -0.1875 to 0.1875
- mesh_out: bfloat16 [512, 512], replicated, may hold values from -0.25 to 0.25
- edge_in: bfloat16 [1024, 512], replicated, may hold values from -0.1875 to 0.1875
- edge_out: bfloat16 [512, 512], replicated, may hold values from -0.25 to 0.25
- node_in: bfloat16 [1024, 512], replicated, may hold values from -0.1875 to 0.1875
- node_out: bfloat16 [512, 512], replicated, may hold values from -0.25 to 0.25
- m2g_in: bfloat16 [1024, 512], replicated, may hold values from -0.1875 to 0.1875
- m2g_out: bfloat16 [512, 512], replicated, may hold values from -0.25 to 0.25
- grid_in: bfloat16 [1024, 512], replicated, may hold values from -0.1875 to 0.1875
- grid_out: bfloat16 [512, 227], replicated, may hold values from -0.25 to 0.25
Outputs:
- increment: bfloat16 [8192, 227], P(('groups', 'lat')), parts along dimension 0
The draws below stay inside these ranges and needn't reach their ends.
There are 2 independent parts, one for each index of `groups`. The reference program is written for one: setup_inputs(seed, part) draws one part's arguments, and reference() takes and returns one part's arrays. A program takes and returns all parts, laid end to end along the dimension named above; an argument that names none is the same for every part. Nothing has to cross between parts.
Inputs may be any that keep to these rules, and one draw needn't show every extreme that they name: `g2m_owner`: each row names 2 different owners; among the 256 rows of one device no owner is named by more than 64 rows, and some owner reaches it. `mm_owner`: each row names 8 different owners; among the 32 rows of one device no owner is named by more than 32 rows, and some owner reaches it. `m2g_owner`: each row names 3 different owners; among the 256 rows of one device no owner is named by more than 96 rows, and some owner reaches it.
All inputs are finite; a program needn't handle non-finite values.
Results may differ from the reference program's by a relative error of at most 0.015.
Values may be sent and summed in bfloat16 or wider, within the bound.
A program may use at most 64 MiB of HBM per device.

```python
import math
import jax
import jax.numpy as jnp
import numpy as np
from jax import lax

C = 227
H = 512
G_DEV = 256
M_DEV = 32
K_G = 2
K_M = 8
K_D = 3
GRID = 4096
MESH = 512
CAP_G = 64
CAP_P = 32
CAP_D = 96
N_LAT = 16


def with_ends(values, own_key, smallest, largest):
    longest = values.shape.index(max(values.shape))
    spots = []
    for shift in (0, 1):
        where = [jax.random.randint(jax.random.fold_in(own_key, axis), (), 0, length) for axis, length in enumerate(values.shape)]
        where[longest] = (where[longest] + shift) % values.shape[longest]
        spots.append(tuple(where))
    return values.at[spots[0]].set(smallest).at[spots[1]].set(largest)


def block_scale(rng, shape, pieces, least, top_value):
    def one(dim, shards_of):
        steps = jax.random.uniform(jax.random.fold_in(jax.random.fold_in(rng, 6), dim), (shards_of,), jnp.float32, least / len(pieces), top_value / len(pieces))
        return jnp.repeat(jnp.exp(steps), shape[dim] // shards_of).reshape((-1,) + (1,) * (len(shape) - dim - 1))

    gain = one(*pieces[0])
    for cut in pieces[1:]:
        gain = gain * one(*cut)
    return gain


def routed_block(own_key, own, number, rows, count, top, bound, slope):
    ranking = jax.random.permutation(own_key, count)
    heavy_load, common = load_shares(count, rows * top, bound, slope, True), load_shares(count, rows * top, bound, slope, False)
    places = jnp.arange(count)

    def named(lengths, offset_by):
        used = int((lengths > 0).sum())
        fixed = max(1, used // 4)
        moved = fixed + (places - fixed + offset_by * (used - fixed)) % max(1, count - fixed)
        return jnp.zeros((count,), jnp.int32).at[ranking[jnp.where(places < fixed, places, moved)]].set(jnp.asarray(lengths, jnp.int32))

    lengths = jnp.where(number % 4 == 0, named(heavy_load, number // 4), named(common, number - number // 4 - 1))
    mixed = jax.random.permutation(jax.random.fold_in(own, 3), count)
    donor, receiver = mixed[0:count // 2 * 2:2], mixed[1:count // 2 * 2:2]
    room = jnp.minimum(lengths[donor] - 1, bound - lengths[receiver]) // 2
    room = jnp.where((donor == ranking[0]) | (receiver == ranking[0]) | (lengths[receiver] == 0), 0, jnp.maximum(room, 0))
    moved = jax.random.randint(jax.random.fold_in(own, 4), (count // 2,), 0, 1 << 20) % (room + 1)
    lengths = lengths.at[donor].add(-moved).at[receiver].add(moved)
    labels = jnp.searchsorted(jnp.cumsum(lengths), jnp.arange(rows * top), side="right").astype(jnp.int32)
    grid = labels.reshape(top, rows).T
    grid = grid[jax.random.permutation(jax.random.fold_in(own, 1), rows)]
    offset_by = jax.random.randint(jax.random.fold_in(own, 2), (rows, 1), 0, top)
    return jnp.take_along_axis(grid, (jnp.arange(top)[None, :] + offset_by) % top, axis=1)


def load_shares(number_of, total, limit, lean, full):
    loads = [(1 << 20) // math.isqrt(grade ** lean) + 1 for grade in range(1, number_of + 1)]
    largest = limit if full else min(limit, max(-(-total // number_of), total * loads[0] // sum(loads)))
    least = 1 if total - largest >= number_of - 1 else 0
    counts, rest = [largest] + [least] * (number_of - 1), total - largest - least * (number_of - 1)
    while rest > 0:
        candidates = [i for i in range(1, number_of) if counts[i] < largest] or [i for i in range(1, number_of) if counts[i] < limit]
        whole, remaining = sum([loads[i] for i in candidates]), rest
        for i in candidates:
            more = min(limit - counts[i], max(1, remaining * loads[i] // whole), rest)
            counts[i] = counts[i] + more
            rest = rest - more
    return np.array(counts)


def scatter_about(stream_key, extent, scale, reach, pieces=(), kind=jnp.bfloat16):
    values = jax.random.normal(stream_key, extent, jnp.float32) * scale
    if len(pieces) > 0:
        values = block_scale(stream_key, extent, pieces, -0.22, 0.18) * values
    return jnp.clip(values, min=-reach, max=reach).astype(kind)


def setup_inputs(seed: int = 0, part: int = 0) -> dict:
    streams_of = jax.random.split(jax.random.key(seed), 23)
    part_splits = jax.random.split(jax.random.fold_in(streams_of[22], part), 23)
    grid_state = scatter_about(part_splits[0], (GRID, C), 1.0, 6.0, ((0, 16),))
    mesh_embed = scatter_about(part_splits[1], (MESH, H), 1.0, 6.0, ((0, 16),))
    g2m_owner_keys = jax.random.split(jax.random.fold_in(part_splits[2], 1), GRID // G_DEV)
    g2m_owner_turns = jax.random.permutation(jax.random.fold_in(part_splits[2], 3), GRID // G_DEV)
    g2m_owner = jax.vmap(lambda own, number: routed_block(jax.random.fold_in(part_splits[2], 2), own, number, G_DEV, N_LAT, K_G, CAP_G, 1))(g2m_owner_keys, g2m_owner_turns).reshape((GRID, K_G))
    g2m_node = with_ends(jax.random.randint(part_splits[3], (GRID, K_G), 0, M_DEV), jax.random.fold_in(part_splits[3], 1), 0, M_DEV - 1).astype(jnp.int32)
    mm_owner_keys = jax.random.split(jax.random.fold_in(part_splits[4], 1), MESH // M_DEV)
    mm_owner_turns = jax.random.permutation(jax.random.fold_in(part_splits[4], 3), MESH // M_DEV)
    mm_owner = jax.vmap(lambda own, number: routed_block(jax.random.fold_in(part_splits[4], 2), own, number, M_DEV, N_LAT, K_M, CAP_P, 1))(mm_owner_keys, mm_owner_turns).reshape((MESH, K_M))
    mm_node = with_ends(jax.random.randint(part_splits[5], (MESH, K_M), 0, M_DEV), jax.random.fold_in(part_splits[5], 1), 0, M_DEV - 1).astype(jnp.int32)
    m2g_owner_keys = jax.random.split(jax.random.fold_in(part_splits[6], 1), GRID // G_DEV)
    m2g_owner_turns = jax.random.permutation(jax.random.fold_in(part_splits[6], 3), GRID // G_DEV)
    m2g_owner = jax.vmap(lambda own, number: routed_block(jax.random.fold_in(part_splits[6], 2), own, number, G_DEV, N_LAT, K_D, CAP_D, 1))(m2g_owner_keys, m2g_owner_turns).reshape((GRID, K_D))
    m2g_node = with_ends(jax.random.randint(part_splits[7], (GRID, K_D), 0, M_DEV), jax.random.fold_in(part_splits[7], 1), 0, M_DEV - 1).astype(jnp.int32)
    embed_in = scatter_about(streams_of[8], (C, H), C ** -0.5, 0.375)
    embed_out = scatter_about(streams_of[9], (H, H), H ** -0.5, 0.25)
    g2m_in = scatter_about(streams_of[10], (2 * H, H), (2 * H) ** -0.5, 0.1875)
    g2m_out = scatter_about(streams_of[11], (H, H), H ** -0.5, 0.25)
    mesh_in = scatter_about(streams_of[12], (2 * H, H), (2 * H) ** -0.5, 0.1875)
    mesh_out = scatter_about(streams_of[13], (H, H), H ** -0.5, 0.25)
    edge_in = scatter_about(streams_of[14], (2 * H, H), (2 * H) ** -0.5, 0.1875)
    edge_out = scatter_about(streams_of[15], (H, H), H ** -0.5, 0.25)
    node_in = scatter_about(streams_of[16], (2 * H, H), (2 * H) ** -0.5, 0.1875)
    node_out = scatter_about(streams_of[17], (H, H), H ** -0.5, 0.25)
    m2g_in = scatter_about(streams_of[18], (2 * H, H), (2 * H) ** -0.5, 0.1875)
    m2g_out = scatter_about(streams_of[19], (H, H), H ** -0.5, 0.25)
    grid_in = scatter_about(streams_of[20], (2 * H, H), (2 * H) ** -0.5, 0.1875)
    grid_out = scatter_about(streams_of[21], (H, C), H ** -0.5, 0.25)
    return dict(grid_state=grid_state, mesh_embed=mesh_embed, g2m_owner=g2m_owner, g2m_node=g2m_node, mm_owner=mm_owner, mm_node=mm_node, m2g_owner=m2g_owner, m2g_node=m2g_node, embed_in=embed_in, embed_out=embed_out, g2m_in=g2m_in, g2m_out=g2m_out, mesh_in=mesh_in, mesh_out=mesh_out, edge_in=edge_in, edge_out=edge_out, node_in=node_in, node_out=node_out, m2g_in=m2g_in, m2g_out=m2g_out, grid_in=grid_in, grid_out=grid_out)


def layer_norm(values):
    center = values - lax.optimization_barrier(jnp.mean(values, axis=-1, keepdims=True))
    spread = lax.optimization_barrier(jnp.mean(center * center, axis=-1, keepdims=True))
    return center * lax.rsqrt(spread + 1e-05)

def mlp_tail(preact, w_out):
    hidden = jax.nn.silu(preact).astype(jnp.bfloat16)
    return layer_norm(jnp.dot(hidden, w_out, preferred_element_type=jnp.float32))

def node_mlp(left, right, w_in, w_out):
    joined = jnp.concatenate([left, right], axis=1)
    return mlp_tail(jnp.dot(joined, w_in, preferred_element_type=jnp.float32), w_out)

def reference(grid_state, mesh_embed, g2m_owner, g2m_node, mm_owner, mm_node, m2g_owner, m2g_node, embed_in, embed_out, g2m_in, g2m_out, mesh_in, mesh_out, edge_in, edge_out, node_in, node_out, m2g_in, m2g_out, grid_in, grid_out):
    grid_latent = mlp_tail(jnp.dot(grid_state, embed_in, preferred_element_type=jnp.float32), embed_out).astype(jnp.bfloat16)
    receivers = (g2m_owner * M_DEV + g2m_node).reshape(-1).astype(jnp.int32)
    sender_part = jnp.dot(grid_latent, g2m_in[:H], preferred_element_type=jnp.float32)
    receiver_part = jnp.dot(mesh_embed, g2m_in[H:], preferred_element_type=jnp.float32)
    preact = jnp.repeat(sender_part, K_G, axis=0) + receiver_part[receivers]
    g2m_message = mlp_tail(preact, g2m_out).astype(jnp.bfloat16)
    g2m_sum = jax.ops.segment_sum(g2m_message.astype(jnp.float32), receivers, num_segments=MESH).astype(jnp.bfloat16)
    mesh_latent = (mesh_embed.astype(jnp.float32) + node_mlp(mesh_embed, g2m_sum, mesh_in, mesh_out)).astype(jnp.bfloat16)
    mesh_senders = (mm_owner * M_DEV + mm_node).reshape(-1).astype(jnp.int32)
    sender_part = jnp.dot(mesh_latent, edge_in[:H], preferred_element_type=jnp.float32)
    receiver_part = jnp.dot(mesh_latent, edge_in[H:], preferred_element_type=jnp.float32)
    preact = sender_part[mesh_senders] + jnp.repeat(receiver_part, K_M, axis=0)
    mesh_message = mlp_tail(preact, edge_out).astype(jnp.bfloat16)
    mesh_sum = lax.optimization_barrier(jnp.sum(mesh_message.astype(jnp.float32).reshape(MESH, K_M, H), axis=1)).astype(jnp.bfloat16)
    mesh_final = (mesh_latent.astype(jnp.float32) + node_mlp(mesh_latent, mesh_sum, node_in, node_out)).astype(jnp.bfloat16)
    grid_senders = (m2g_owner * M_DEV + m2g_node).reshape(-1).astype(jnp.int32)
    sender_part = jnp.dot(mesh_final, m2g_in[:H], preferred_element_type=jnp.float32)
    receiver_part = jnp.dot(grid_latent, m2g_in[H:], preferred_element_type=jnp.float32)
    preact = sender_part[grid_senders] + jnp.repeat(receiver_part, K_D, axis=0)
    m2g_message = mlp_tail(preact, m2g_out).astype(jnp.bfloat16)
    m2g_sum = lax.optimization_barrier(jnp.sum(m2g_message.astype(jnp.float32).reshape(GRID, K_D, H), axis=1)).astype(jnp.bfloat16)
    joined = jnp.concatenate([grid_latent, m2g_sum], axis=1)
    grid_hidden = jax.nn.silu(jnp.dot(joined, grid_in, preferred_element_type=jnp.float32)).astype(jnp.bfloat16)
    return jnp.dot(grid_hidden, grid_out, preferred_element_type=jnp.float32).astype(jnp.bfloat16)
```

```python
import functools

import jax
import jax.numpy as jnp
from jax import lax
from jax.experimental import pallas as pl
from jax.experimental.pallas import tpu as pltpu
from jax.sharding import PartitionSpec as P

BF16 = jnp.bfloat16
F32 = jnp.float32


def layer_norm(values):
    center = values - jnp.mean(values, axis=-1, keepdims=True)
    spread = jnp.mean(center * center, axis=-1, keepdims=True)
    return center * lax.rsqrt(spread + 1e-05)


def mlp_tail(preact, w_out):
    hidden = jax.nn.silu(preact).astype(jnp.bfloat16)
    return layer_norm(jnp.dot(hidden, w_out, preferred_element_type=jnp.float32))


def node_mlp(left, right, w_in, w_out):
    joined = jnp.concatenate([left, right], axis=1)
    return mlp_tail(jnp.dot(joined, w_in, preferred_element_type=jnp.float32), w_out)


def slot_index(owners, capacity):
    total = owners.shape[0]
    position = jnp.arange(total, dtype=jnp.int32)
    matches = (owners[:, None] == owners[None, :]) & (position[None, :] < position[:, None])
    return owners * capacity + jnp.sum(matches.astype(jnp.int32), axis=1)


def capacity_of(edge_count, peer_count):
    return max(2, (2 * edge_count + peer_count - 1) // peer_count)


def body(
    grid_state,
    mesh_embed,
    g2m_owner,
    g2m_node,
    mm_owner,
    mm_node,
    m2g_owner,
    m2g_node,
    embed_in,
    embed_out,
    g2m_in,
    g2m_out,
    mesh_in,
    mesh_out,
    edge_in,
    edge_out,
    node_in,
    node_out,
    m2g_in,
    m2g_out,
    grid_in,
    grid_out,
):
    peer_count = lax.axis_size("lat")
    latent_width = embed_out.shape[1]
    grid_rows = grid_state.shape[0]
    mesh_rows = mesh_embed.shape[0]
    grid_latent = mlp_tail(
        jnp.dot(grid_state, embed_in, preferred_element_type=jnp.float32), embed_out
    ).astype(jnp.bfloat16)
    fan_grid = g2m_owner.shape[1]
    cap_grid = capacity_of(grid_rows * fan_grid, peer_count)
    grid_slots = slot_index(g2m_owner.reshape(-1), cap_grid)
    outgoing = jnp.repeat(grid_latent, fan_grid, axis=0)
    send_rows = (
        jnp.zeros((peer_count * cap_grid, latent_width), jnp.bfloat16).at[grid_slots].set(outgoing)
    )
    send_rows = send_rows.reshape(peer_count, cap_grid, latent_width)
    send_nodes = (
        jnp.full((peer_count * cap_grid,), mesh_rows, jnp.int32)
        .at[grid_slots]
        .set(g2m_node.reshape(-1))
    )
    send_nodes = send_nodes.reshape(peer_count, cap_grid)
    receiver_part = jnp.dot(mesh_embed, g2m_in[latent_width:], preferred_element_type=jnp.float32)
    receiver_padded = jnp.concatenate(
        [receiver_part, jnp.zeros((1, latent_width), jnp.float32)], axis=0
    )
    slot_rows = lax.all_to_all(send_rows, "lat", split_axis=0, concat_axis=0, tiled=True)
    slot_nodes = lax.all_to_all(send_nodes, "lat", split_axis=0, concat_axis=0, tiled=True)
    preact = jnp.einsum(
        "pch,hk->pck", slot_rows, g2m_in[:latent_width], preferred_element_type=jnp.float32
    )
    preact = preact + receiver_padded[slot_nodes]
    hidden = jax.nn.silu(preact).astype(jnp.bfloat16)
    result = jnp.einsum("pch,hk->pck", hidden, g2m_out, preferred_element_type=jnp.float32)
    arrived = layer_norm(result).astype(jnp.bfloat16)
    one_hot = (
        slot_nodes.reshape(-1)[:, None] == jnp.arange(mesh_rows, dtype=jnp.int32)[None, :]
    ).astype(jnp.bfloat16)
    g2m_sum = jnp.einsum(
        "rm,rh->mh", one_hot, arrived.reshape(-1, latent_width), preferred_element_type=jnp.float32
    ).astype(jnp.bfloat16)
    mesh_latent = (
        mesh_embed.astype(jnp.float32) + node_mlp(mesh_embed, g2m_sum, mesh_in, mesh_out)
    ).astype(jnp.bfloat16)
    fan_mesh = mm_owner.shape[1]
    every_mesh = lax.all_gather(mesh_latent, "lat", axis=0, tiled=True)
    mesh_senders = every_mesh[(mm_owner * mesh_rows + mm_node).reshape(-1)]
    receiver_mesh = jnp.dot(mesh_latent, edge_in[latent_width:], preferred_element_type=jnp.float32)
    preact = jnp.dot(mesh_senders, edge_in[:latent_width], preferred_element_type=jnp.float32)
    preact = preact + jnp.repeat(receiver_mesh, fan_mesh, axis=0)
    mesh_message = mlp_tail(preact, edge_out).astype(jnp.bfloat16)
    mesh_sum = jnp.sum(
        mesh_message.astype(jnp.float32).reshape(mesh_rows, fan_mesh, latent_width), axis=1
    ).astype(jnp.bfloat16)
    mesh_final = (
        mesh_latent.astype(jnp.float32) + node_mlp(mesh_latent, mesh_sum, node_in, node_out)
    ).astype(jnp.bfloat16)
    fan_down = m2g_owner.shape[1]
    every_final = lax.all_gather(mesh_final, "lat", axis=0, tiled=True)
    grid_senders = every_final[(m2g_owner * mesh_rows + m2g_node).reshape(-1)]
    receiver_grid = jnp.dot(grid_latent, m2g_in[latent_width:], preferred_element_type=jnp.float32)
    preact = jnp.dot(grid_senders, m2g_in[:latent_width], preferred_element_type=jnp.float32)
    preact = preact + jnp.repeat(receiver_grid, fan_down, axis=0)
    down_message = mlp_tail(preact, m2g_out).astype(jnp.bfloat16)
    down_sum = jnp.sum(
        down_message.astype(jnp.float32).reshape(grid_rows, fan_down, latent_width), axis=1
    ).astype(jnp.bfloat16)
    joined = jnp.concatenate([grid_latent, down_sum], axis=1)
    grid_hidden = jax.nn.silu(jnp.dot(joined, grid_in, preferred_element_type=jnp.float32)).astype(
        jnp.bfloat16
    )
    return jnp.dot(grid_hidden, grid_out, preferred_element_type=jnp.float32).astype(jnp.bfloat16)


def dot(a, b):
    return jnp.dot(a, b, preferred_element_type=F32)


def dot_lhs_t(a, b):
    return lax.dot_general(a, b, (((0,), (0,)), ((), ())), preferred_element_type=F32)


def dot_rhs_t(a, b):
    return lax.dot_general(a, b, (((1,), (1,)), ((), ())), preferred_element_type=F32)


def silu(v):
    half = 0.5 * v
    return half + half * jnp.tanh(half)


def tail(preact, w_out):
    return layer_norm(dot(silu(preact).astype(BF16), w_out))


WEIGHTS = 13


def fused(depth, *refs):
    state, embed, g2m_o, g2m_n, mm_o, mm_n, m2g_o, m2g_n, grid_out = refs[:9]
    hbm = refs[9 : 9 + WEIGHTS]
    out = refs[9 + WEIGHTS]
    scratch = refs[10 + WEIGHTS :]
    vmem = scratch[:WEIGHTS]
    (buf1, buf2, buf3, part, got1, sum2, got2, sum3, got3, down_recv, grid_part, state_pad, embed_pad) = scratch[
        WEIGHTS : WEIGHTS + 13
    ]
    (load_sem, send1, recv1, send2, recv2, send3, recv3, cs, cr, xs, xr, zs, zr) = scratch[
        WEIGHTS + 13 :
    ]
    me = lax.axis_index("lat")
    z, x, c = me // 4, (me // 2) % 2, me % 2
    rows, width = embed.shape
    channels = state.shape[0]
    count = 4 * depth

    def at(zz, xx, cc):
        return (zz * 2 + xx) * 2 + cc

    def block(zz, xx, cc):
        return (cc * 2 + xx) * depth + zz

    def away(d):
        return (z + d) % depth

    def put(src, dst, send, recv, target):
        return pltpu.make_async_remote_copy(
            src_ref=src,
            dst_ref=dst,
            send_sem=send,
            recv_sem=recv,
            device_id={"lat": target},
            device_id_type=pl.DeviceIdType.MESH,
        )

    loads = [pltpu.make_async_copy(h, v, load_sem.at[i]) for i, (h, v) in enumerate(zip(hbm, vmem))]
    (embed_in, embed_out, g2m_in, g2m_out, mesh_in, mesh_out, edge_in, edge_out, node_in, node_out, m2g_in, m2g_out, grid_in) = vmem
    barrier = pltpu.get_barrier_semaphore()
    partners = [at(away(d), x, c) for d in range(1, depth)] + [at(z, 1 - x, c), at(z, x, 1 - c)]
    for partner in partners:
        pl.semaphore_signal(
            barrier, inc=1, device_id={"lat": partner}, device_id_type=pl.DeviceIdType.MESH
        )
    for load in loads:
        load.start()

    class Gather:
        def __init__(self, buf, send, recv):
            self.buf, self.send, self.recv, self.sent = buf, send, recv, []

        def copy(self, q, target):
            n = len(self.sent)
            made = put(self.buf.at[q], self.buf.at[q], self.send.at[n], self.recv.at[q], target)
            made.start()
            self.sent.append(made)

        def arrive(self, q):
            put(self.buf.at[q], self.buf.at[q], self.send.at[0], self.recv.at[q], me).wait_recv()

        def begin(self, values):
            own = block(z, x, c)
            self.buf[own] = values
            self.copy(own, at(z, 1 - x, c))
            for d in range(1, depth):
                self.copy(own, at(away(d), x, c))
            self.copy(own, at(z, x, 1 - c))

        def forward(self):
            for d in range(1, depth):
                q = block(away(d), x, c)
                self.arrive(q)
                self.copy(q, at(z, 1 - x, c))
                self.copy(q, at(z, x, 1 - c))

        def cross(self):
            for d in range(depth):
                q = block(away(d), 1 - x, c)
                self.arrive(q)
                self.copy(q, at(z, x, 1 - c))

        def finish(self):
            for xx in (x, 1 - x):
                for d in range(depth):
                    self.arrive(block(away(d), xx, 1 - c))

        def rows(self):
            return self.buf[...].reshape(count * rows, width)

        def drain(self):
            for made in self.sent:
                made.wait_send()

    def place(owner, node):
        return (((owner & 1) * 2 + ((owner >> 1) & 1)) * depth + (owner >> 2)) * rows + node

    def picks(column):
        lanes = lax.broadcasted_iota(jnp.int32, (column.shape[0], count * rows), 1)
        return (lanes == column).astype(F32).astype(BF16)

    g2m_at = place(g2m_o[...], g2m_n[...])
    g2m_t = jnp.transpose(g2m_at)
    fan_grid = g2m_at.shape[0]

    own_rows = embed[...]
    first = Gather(buf1, send1, recv1)
    pl.semaphore_wait(barrier, len(partners))
    first.begin(own_rows)

    loads[0].wait()
    loads[1].wait()
    whole = channels // 16 * 16
    for padded, source in ((state_pad, state), (embed_pad, embed_in)):
        padded[whole:] = jnp.zeros((padded.shape[0] - whole, padded.shape[1]), BF16)
        padded[:channels] = source[...]
    latent = tail(dot_lhs_t(state_pad[...], embed_pad[...]), embed_out[...]).astype(BF16)
    first.forward()
    loads[2].wait()
    sender = dot(latent, g2m_in[:width])
    first.cross()
    loads[3].wait()
    loads[4].wait()
    mesh_part = dot(own_rows, mesh_in[:width])
    first.finish()
    every = first.rows()
    messages = []
    for k in range(fan_grid):
        picked = dot(picks(g2m_t[:, k : k + 1]), every).astype(BF16)
        messages.append(tail(sender + dot(picked, g2m_in[width:]), g2m_out[...]).astype(BF16))

    def partial(xx, cc):
        span = depth * rows
        places = lax.broadcasted_iota(jnp.int32, (span, g2m_at.shape[1]), 0) + (cc * 2 + xx) * span
        total = jnp.zeros((span, width), F32)
        for k in range(fan_grid):
            hits = (places == g2m_at[k : k + 1, :]).astype(F32).astype(BF16)
            total = total + dot(hits, messages[k])
        return total.reshape(depth, rows, width)

    def group(xx, cc):
        return pl.ds((cc * 2 + xx) * depth, depth)

    sends = []
    for n, xx in enumerate((1 - x, x)):
        part[group(xx, 1 - c)] = partial(xx, 1 - c).astype(BF16)
        made = put(
            part.at[group(xx, 1 - c)],
            got1.at[n],
            cs.at[n],
            cr.at[n],
            at(z, x, 1 - c),
        )
        made.start()
        sends.append(made)
    cross_part = partial(1 - x, c)
    part[group(x, c)] = partial(x, c).astype(BF16)
    sends[0].wait_recv()
    sum2[...] = (cross_part + got1[0].astype(F32)).astype(BF16)
    for d in list(range(1, depth)) + [0]:
        zz = away(d)
        made = put(sum2.at[zz], got2.at[zz], xs.at[zz], xr.at[zz], at(z, 1 - x, c))
        made.start()
        sends.append(made)
    sends[1].wait_recv()

    def ready(zz):
        put(sum2.at[zz], got2.at[zz], xs.at[zz], xr.at[zz], at(z, 1 - x, c)).wait_recv()
        return (
            part[block(zz, x, c)].astype(F32) + got1[1, zz].astype(F32) + got2[zz].astype(F32)
        )

    for d in range(1, depth):
        zz = away(d)
        sum3[zz] = ready(zz).astype(BF16)
        made = put(sum3.at[zz], got3.at[z], zs.at[zz], zr.at[z], at(zz, x, c))
        made.start()
        sends.append(made)
    g2m_sum = ready(z)
    for d in range(1, depth):
        zz = away(d)
        put(sum3.at[zz], got3.at[zz], zs.at[zz], zr.at[zz], at(zz, x, c)).wait_recv()
        g2m_sum = g2m_sum + got3[zz].astype(F32)
    loads[5].wait()
    mesh_latent = (
        own_rows.astype(F32)
        + tail(mesh_part + dot(g2m_sum.astype(BF16), mesh_in[width:]), mesh_out[...])
    ).astype(BF16)

    second = Gather(buf2, send2, recv2)
    second.begin(mesh_latent)
    loads[6].wait()
    loads[8].wait()
    receiver = dot(mesh_latent, edge_in[width:])
    node_part = dot(mesh_latent, node_in[:width])
    second.forward()
    loads[10].wait()
    down_recv[...] = dot(latent, m2g_in[width:])
    second.cross()
    loads[12].wait()
    grid_part[...] = dot(latent, grid_in[:width])
    mm_t = jnp.transpose(place(mm_o[...], mm_n[...]))
    fan_mesh = mm_t.shape[1]
    mm_picks = jnp.concatenate([picks(mm_t[:, k : k + 1]) for k in range(fan_mesh)], axis=0)
    loads[7].wait()
    second.finish()
    picked = dot(mm_picks, second.rows()).astype(BF16)
    preact = receiver[None] + dot(picked, edge_in[:width]).reshape(fan_mesh, rows, width)
    message = tail(preact.reshape(fan_mesh * rows, width), edge_out[...]).astype(BF16)
    mesh_sum = jnp.sum(message.astype(F32).reshape(fan_mesh, rows, width), axis=0)
    loads[9].wait()
    mesh_final = (
        mesh_latent.astype(F32)
        + tail(node_part + dot(mesh_sum.astype(BF16), node_in[width:]), node_out[...])
    ).astype(BF16)

    third = Gather(buf3, send3, recv3)
    third.begin(mesh_final)
    m2g_t = jnp.transpose(place(m2g_o[...], m2g_n[...]))
    fan_down = m2g_t.shape[1]
    loads[11].wait()
    third.forward()
    third.cross()
    third.finish()
    every = third.rows()
    down_sum = None
    for k in range(fan_down):
        picked = dot(picks(m2g_t[:, k : k + 1]), every).astype(BF16)
        message = tail(down_recv[...] + dot(picked, m2g_in[:width]), m2g_out[...])
        message = message.astype(BF16).astype(F32)
        down_sum = message if down_sum is None else down_sum + message
    hidden = silu(grid_part[...] + dot(down_sum.astype(BF16), grid_in[width:])).astype(BF16)
    out[...] = dot_rhs_t(grid_out[...], hidden).astype(BF16)
    for made in sends:
        made.wait_send()
    for gather in (first, second, third):
        gather.drain()


def fused_body(*args):
    state, embed, *rest = args
    indices, weights = rest[:6], rest[6:]
    lat = lax.axis_size("lat")
    depth = lat // 4
    rows, width = embed.shape
    grid_rows, channels = state.shape
    vmem_spec = pl.BlockSpec(memory_space=pltpu.VMEM)
    hbm_spec = pl.BlockSpec(memory_space=pltpu.HBM)
    channel_pad = -(-channels // 128) * 128
    dma = pltpu.SemaphoreType.DMA
    gather_sems = [dma((4 * depth,)), dma((lat,))]
    result = pl.pallas_call(
        functools.partial(fused, depth),
        out_shape=jax.ShapeDtypeStruct((channels, grid_rows), BF16),
        in_specs=[vmem_spec] * 9 + [hbm_spec] * WEIGHTS,
        out_specs=vmem_spec,
        scratch_shapes=[pltpu.VMEM(w.shape, w.dtype) for w in weights[:WEIGHTS]]
        + [pltpu.VMEM((lat, rows, width), BF16)] * 4
        + [pltpu.VMEM((2, depth, rows, width), BF16)]
        + [pltpu.VMEM((depth, rows, width), BF16)] * 4
        + [pltpu.VMEM((grid_rows, width), F32)] * 2
        + [pltpu.VMEM((channel_pad, grid_rows), BF16), pltpu.VMEM((channel_pad, width), BF16)]
        + [dma((WEIGHTS,))]
        + gather_sems * 3
        + [dma((2,))] * 2
        + [dma((depth,))] * 4,
        compiler_params=pltpu.CompilerParams(
            collective_id=0, has_side_effects=True, vmem_limit_bytes=63 * 1024 * 1024
        ),
        cost_estimate=pl.CostEstimate(flops=2 * 10**9, bytes_accessed=10**7, transcendentals=10**6),
    )(state.T, embed, *[i.T for i in indices], weights[WEIGHTS].T, *weights[:WEIGHTS])
    return result.T


def solution(mesh):
    lat = mesh.shape["lat"]
    step = fused_body if lat % 4 == 0 and 8 <= lat <= 32 else body
    in_specs = (
        P(("groups", "lat"), None),
        P(("groups", "lat"), None),
        P(("groups", "lat"), None),
        P(("groups", "lat"), None),
        P(("groups", "lat"), None),
        P(("groups", "lat"), None),
        P(("groups", "lat"), None),
        P(("groups", "lat"), None),
        P(),
        P(),
        P(),
        P(),
        P(),
        P(),
        P(),
        P(),
        P(),
        P(),
        P(),
        P(),
        P(),
        P(),
    )
    out_specs = P(("groups", "lat"), None)
    return jax.shard_map(step, mesh=mesh, in_specs=in_specs, out_specs=out_specs, check_vma=False)
```

```python
import functools

import jax
import jax.numpy as jnp
from jax import lax
from jax.experimental import pallas as pl
from jax.experimental.pallas import tpu as pltpu
from jax.sharding import PartitionSpec as P

BF16 = jnp.bfloat16
F32 = jnp.float32


def layer_norm(values):
    center = values - jnp.mean(values, axis=-1, keepdims=True)
    spread = jnp.mean(center * center, axis=-1, keepdims=True)
    return center * lax.rsqrt(spread + 1e-05)


def mlp_tail(preact, w_out):
    hidden = jax.nn.silu(preact).astype(jnp.bfloat16)
    return layer_norm(jnp.dot(hidden, w_out, preferred_element_type=jnp.float32))


def node_mlp(left, right, w_in, w_out):
    joined = jnp.concatenate([left, right], axis=1)
    return mlp_tail(jnp.dot(joined, w_in, preferred_element_type=jnp.float32), w_out)


def slot_index(owners, capacity):
    total = owners.shape[0]
    position = jnp.arange(total, dtype=jnp.int32)
    matches = (owners[:, None] == owners[None, :]) & (position[None, :] < position[:, None])
    return owners * capacity + jnp.sum(matches.astype(jnp.int32), axis=1)


def capacity_of(edge_count, peer_count):
    return max(2, (2 * edge_count + peer_count - 1) // peer_count)


def body(
    grid_state,
    mesh_embed,
    g2m_owner,
    g2m_node,
    mm_owner,
    mm_node,
    m2g_owner,
    m2g_node,
    embed_in,
    embed_out,
    g2m_in,
    g2m_out,
    mesh_in,
    mesh_out,
    edge_in,
    edge_out,
    node_in,
    node_out,
    m2g_in,
    m2g_out,
    grid_in,
    grid_out,
):
    peer_count = lax.axis_size("lat")
    latent_width = embed_out.shape[1]
    grid_rows = grid_state.shape[0]
    mesh_rows = mesh_embed.shape[0]
    grid_latent = mlp_tail(
        jnp.dot(grid_state, embed_in, preferred_element_type=jnp.float32), embed_out
    ).astype(jnp.bfloat16)
    fan_grid = g2m_owner.shape[1]
    cap_grid = capacity_of(grid_rows * fan_grid, peer_count)
    grid_slots = slot_index(g2m_owner.reshape(-1), cap_grid)
    outgoing = jnp.repeat(grid_latent, fan_grid, axis=0)
    send_rows = (
        jnp.zeros((peer_count * cap_grid, latent_width), jnp.bfloat16).at[grid_slots].set(outgoing)
    )
    send_rows = send_rows.reshape(peer_count, cap_grid, latent_width)
    send_nodes = (
        jnp.full((peer_count * cap_grid,), mesh_rows, jnp.int32)
        .at[grid_slots]
        .set(g2m_node.reshape(-1))
    )
    send_nodes = send_nodes.reshape(peer_count, cap_grid)
    receiver_part = jnp.dot(mesh_embed, g2m_in[latent_width:], preferred_element_type=jnp.float32)
    receiver_padded = jnp.concatenate(
        [receiver_part, jnp.zeros((1, latent_width), jnp.float32)], axis=0
    )
    slot_rows = lax.all_to_all(send_rows, "lat", split_axis=0, concat_axis=0, tiled=True)
    slot_nodes = lax.all_to_all(send_nodes, "lat", split_axis=0, concat_axis=0, tiled=True)
    preact = jnp.einsum(
        "pch,hk->pck", slot_rows, g2m_in[:latent_width], preferred_element_type=jnp.float32
    )
    preact = preact + receiver_padded[slot_nodes]
    hidden = jax.nn.silu(preact).astype(jnp.bfloat16)
    result = jnp.einsum("pch,hk->pck", hidden, g2m_out, preferred_element_type=jnp.float32)
    arrived = layer_norm(result).astype(jnp.bfloat16)
    one_hot = (
        slot_nodes.reshape(-1)[:, None] == jnp.arange(mesh_rows, dtype=jnp.int32)[None, :]
    ).astype(jnp.bfloat16)
    g2m_sum = jnp.einsum(
        "rm,rh->mh", one_hot, arrived.reshape(-1, latent_width), preferred_element_type=jnp.float32
    ).astype(jnp.bfloat16)
    mesh_latent = (
        mesh_embed.astype(jnp.float32) + node_mlp(mesh_embed, g2m_sum, mesh_in, mesh_out)
    ).astype(jnp.bfloat16)
    fan_mesh = mm_owner.shape[1]
    every_mesh = lax.all_gather(mesh_latent, "lat", axis=0, tiled=True)
    mesh_senders = every_mesh[(mm_owner * mesh_rows + mm_node).reshape(-1)]
    receiver_mesh = jnp.dot(mesh_latent, edge_in[latent_width:], preferred_element_type=jnp.float32)
    preact = jnp.dot(mesh_senders, edge_in[:latent_width], preferred_element_type=jnp.float32)
    preact = preact + jnp.repeat(receiver_mesh, fan_mesh, axis=0)
    mesh_message = mlp_tail(preact, edge_out).astype(jnp.bfloat16)
    mesh_sum = jnp.sum(
        mesh_message.astype(jnp.float32).reshape(mesh_rows, fan_mesh, latent_width), axis=1
    ).astype(jnp.bfloat16)
    mesh_final = (
        mesh_latent.astype(jnp.float32) + node_mlp(mesh_latent, mesh_sum, node_in, node_out)
    ).astype(jnp.bfloat16)
    fan_down = m2g_owner.shape[1]
    every_final = lax.all_gather(mesh_final, "lat", axis=0, tiled=True)
    grid_senders = every_final[(m2g_owner * mesh_rows + m2g_node).reshape(-1)]
    receiver_grid = jnp.dot(grid_latent, m2g_in[latent_width:], preferred_element_type=jnp.float32)
    preact = jnp.dot(grid_senders, m2g_in[:latent_width], preferred_element_type=jnp.float32)
    preact = preact + jnp.repeat(receiver_grid, fan_down, axis=0)
    down_message = mlp_tail(preact, m2g_out).astype(jnp.bfloat16)
    down_sum = jnp.sum(
        down_message.astype(jnp.float32).reshape(grid_rows, fan_down, latent_width), axis=1
    ).astype(jnp.bfloat16)
    joined = jnp.concatenate([grid_latent, down_sum], axis=1)
    grid_hidden = jax.nn.silu(jnp.dot(joined, grid_in, preferred_element_type=jnp.float32)).astype(
        jnp.bfloat16
    )
    return jnp.dot(grid_hidden, grid_out, preferred_element_type=jnp.float32).astype(jnp.bfloat16)


def dot(a, b):
    return jnp.dot(a, b, preferred_element_type=F32)


def dot_lhs_t(a, b):
    return lax.dot_general(a, b, (((0,), (0,)), ((), ())), preferred_element_type=F32)


def dot_rhs_t(a, b):
    return lax.dot_general(a, b, (((1,), (1,)), ((), ())), preferred_element_type=F32)


def silu(v):
    half = 0.5 * v
    return half + half * jnp.tanh(half)


def tail(preact, w_out):
    return layer_norm(dot(silu(preact).astype(BF16), w_out))


WEIGHTS = 13


def fused(depth, *refs):
    state, embed, g2m_o, g2m_n, mm_o, mm_n, m2g_o, m2g_n, grid_out = refs[:9]
    hbm = refs[9 : 9 + WEIGHTS]
    out = refs[9 + WEIGHTS]
    scratch = refs[10 + WEIGHTS :]
    vmem = scratch[:WEIGHTS]
    (buf1, buf2, buf3, part, got1, sum2, got2, sum3, got3, down_recv, grid_part, state_pad, embed_pad) = scratch[
        WEIGHTS : WEIGHTS + 13
    ]
    (load_sem, send1, recv1, send2, recv2, send3, recv3, cs, cr, xs, xr, zs, zr) = scratch[
        WEIGHTS + 13 :
    ]
    me = lax.axis_index("lat")
    z, x, c = me // 4, (me // 2) % 2, me % 2
    rows, width = embed.shape
    channels = state.shape[0]
    count = 4 * depth

    def at(zz, xx, cc):
        return (zz * 2 + xx) * 2 + cc

    def block(zz, xx, cc):
        return (cc * 2 + xx) * depth + zz

    def away(d):
        return (z + d) % depth

    def put(src, dst, send, recv, target):
        return pltpu.make_async_remote_copy(
            src_ref=src,
            dst_ref=dst,
            send_sem=send,
            recv_sem=recv,
            device_id={"lat": target},
            device_id_type=pl.DeviceIdType.MESH,
        )

    loads = [pltpu.make_async_copy(h, v, load_sem.at[i]) for i, (h, v) in enumerate(zip(hbm, vmem))]
    (embed_in, embed_out, g2m_in, g2m_out, mesh_in, mesh_out, edge_in, edge_out, node_in, node_out, m2g_in, m2g_out, grid_in) = vmem
    barrier = pltpu.get_barrier_semaphore()
    partners = [at(away(d), xx, c) for d in range(1, depth) for xx in (x, 1 - x)] + [at(z, 1 - x, c), at(z, x, 1 - c)]
    for partner in partners:
        pl.semaphore_signal(
            barrier, inc=1, device_id={"lat": partner}, device_id_type=pl.DeviceIdType.MESH
        )
    for load in loads:
        load.start()

    class Gather:
        def __init__(self, buf, send, recv):
            self.buf, self.send, self.recv, self.sent = buf, send, recv, []

        def copy(self, q, target):
            n = len(self.sent)
            made = put(self.buf.at[q], self.buf.at[q], self.send.at[n], self.recv.at[q], target)
            made.start()
            self.sent.append(made)

        def arrive(self, q):
            put(self.buf.at[q], self.buf.at[q], self.send.at[0], self.recv.at[q], me).wait_recv()

        def begin(self, values):
            own = block(z, x, c)
            self.buf[own] = values
            for d in range(1, depth):
                self.copy(own, at(away(d), 1 - x, c))
                self.copy(own, at(away(d), x, c))
            self.copy(own, at(z, 1 - x, c))
            self.copy(own, at(z, x, 1 - c))

        def forward(self):
            q = block(z, 1 - x, c)
            self.arrive(q)
            self.copy(q, at(z, x, 1 - c))

        def cross(self):
            for d in range(1, depth):
                for xx in (x, 1 - x):
                    q = block(away(d), xx, c)
                    self.arrive(q)
                    self.copy(q, at(z, x, 1 - c))

        def finish(self):
            for xx in (x, 1 - x):
                for d in range(depth):
                    self.arrive(block(away(d), xx, 1 - c))

        def rows(self):
            return self.buf[...].reshape(count * rows, width)

        def drain(self):
            for made in self.sent:
                made.wait_send()

    def place(owner, node):
        return (((owner & 1) * 2 + ((owner >> 1) & 1)) * depth + (owner >> 2)) * rows + node

    def picks(column):
        lanes = lax.broadcasted_iota(jnp.int32, (column.shape[0], count * rows), 1)
        return (lanes == column).astype(F32).astype(BF16)

    g2m_at = place(g2m_o[...], g2m_n[...])
    g2m_t = jnp.transpose(g2m_at)
    fan_grid = g2m_at.shape[0]

    own_rows = embed[...]
    first = Gather(buf1, send1, recv1)
    pl.semaphore_wait(barrier, len(partners))
    first.begin(own_rows)

    loads[0].wait()
    loads[1].wait()
    whole = channels // 16 * 16
    for padded, source in ((state_pad, state), (embed_pad, embed_in)):
        padded[whole:] = jnp.zeros((padded.shape[0] - whole, padded.shape[1]), BF16)
        padded[:channels] = source[...]
    latent = tail(dot_lhs_t(state_pad[...], embed_pad[...]), embed_out[...]).astype(BF16)
    first.forward()
    loads[2].wait()
    sender = dot(latent, g2m_in[:width])
    first.cross()
    loads[3].wait()
    loads[4].wait()
    mesh_part = dot(own_rows, mesh_in[:width])
    first.finish()
    every = first.rows()
    messages = []
    for k in range(fan_grid):
        picked = dot(picks(g2m_t[:, k : k + 1]), every).astype(BF16)
        messages.append(tail(sender + dot(picked, g2m_in[width:]), g2m_out[...]).astype(BF16))

    def partial(xx, cc):
        span = depth * rows
        places = lax.broadcasted_iota(jnp.int32, (span, g2m_at.shape[1]), 0) + (cc * 2 + xx) * span
        total = jnp.zeros((span, width), F32)
        for k in range(fan_grid):
            hits = (places == g2m_at[k : k + 1, :]).astype(F32).astype(BF16)
            total = total + dot(hits, messages[k])
        return total.reshape(depth, rows, width)

    def group(xx, cc):
        return pl.ds((cc * 2 + xx) * depth, depth)

    sends = []
    for n, xx in enumerate((1 - x, x)):
        part[group(xx, 1 - c)] = partial(xx, 1 - c).astype(BF16)
        made = put(
            part.at[group(xx, 1 - c)],
            got1.at[n],
            cs.at[n],
            cr.at[n],
            at(z, x, 1 - c),
        )
        made.start()
        sends.append(made)
    cross_part = partial(1 - x, c)
    part[group(x, c)] = partial(x, c).astype(BF16)
    sends[0].wait_recv()
    sum2[...] = (cross_part + got1[0].astype(F32)).astype(BF16)
    for d in list(range(1, depth)) + [0]:
        zz = away(d)
        made = put(sum2.at[zz], got2.at[zz], xs.at[zz], xr.at[zz], at(z, 1 - x, c))
        made.start()
        sends.append(made)
    sends[1].wait_recv()

    def ready(zz):
        put(sum2.at[zz], got2.at[zz], xs.at[zz], xr.at[zz], at(z, 1 - x, c)).wait_recv()
        return (
            part[block(zz, x, c)].astype(F32) + got1[1, zz].astype(F32) + got2[zz].astype(F32)
        )

    for d in range(1, depth):
        zz = away(d)
        sum3[zz] = ready(zz).astype(BF16)
        made = put(sum3.at[zz], got3.at[z], zs.at[zz], zr.at[z], at(zz, x, c))
        made.start()
        sends.append(made)
    g2m_sum = ready(z)
    for d in range(1, depth):
        zz = away(d)
        put(sum3.at[zz], got3.at[zz], zs.at[zz], zr.at[zz], at(zz, x, c)).wait_recv()
        g2m_sum = g2m_sum + got3[zz].astype(F32)
    loads[5].wait()
    mesh_latent = (
        own_rows.astype(F32)
        + tail(mesh_part + dot(g2m_sum.astype(BF16), mesh_in[width:]), mesh_out[...])
    ).astype(BF16)

    second = Gather(buf2, send2, recv2)
    second.begin(mesh_latent)
    loads[6].wait()
    loads[8].wait()
    receiver = dot(mesh_latent, edge_in[width:])
    node_part = dot(mesh_latent, node_in[:width])
    second.forward()
    loads[10].wait()
    down_recv[...] = dot(latent, m2g_in[width:])
    second.cross()
    loads[12].wait()
    grid_part[...] = dot(latent, grid_in[:width])
    mm_t = jnp.transpose(place(mm_o[...], mm_n[...]))
    fan_mesh = mm_t.shape[1]
    mm_picks = jnp.concatenate([picks(mm_t[:, k : k + 1]) for k in range(fan_mesh)], axis=0)
    loads[7].wait()
    second.finish()
    picked = dot(mm_picks, second.rows()).astype(BF16)
    preact = receiver[None] + dot(picked, edge_in[:width]).reshape(fan_mesh, rows, width)
    message = tail(preact.reshape(fan_mesh * rows, width), edge_out[...]).astype(BF16)
    mesh_sum = jnp.sum(message.astype(F32).reshape(fan_mesh, rows, width), axis=0)
    loads[9].wait()
    mesh_final = (
        mesh_latent.astype(F32)
        + tail(node_part + dot(mesh_sum.astype(BF16), node_in[width:]), node_out[...])
    ).astype(BF16)

    third = Gather(buf3, send3, recv3)
    third.begin(mesh_final)
    m2g_t = jnp.transpose(place(m2g_o[...], m2g_n[...]))
    fan_down = m2g_t.shape[1]
    loads[11].wait()
    third.forward()
    third.cross()
    third.finish()
    every = third.rows()
    down_sum = None
    for k in range(fan_down):
        picked = dot(picks(m2g_t[:, k : k + 1]), every).astype(BF16)
        message = tail(down_recv[...] + dot(picked, m2g_in[:width]), m2g_out[...])
        message = message.astype(BF16).astype(F32)
        down_sum = message if down_sum is None else down_sum + message
    hidden = silu(grid_part[...] + dot(down_sum.astype(BF16), grid_in[width:])).astype(BF16)
    out[...] = dot_rhs_t(grid_out[...], hidden).astype(BF16)
    for made in sends:
        made.wait_send()
    for gather in (first, second, third):
        gather.drain()


def fused_body(*args):
    state, embed, *rest = args
    indices, weights = rest[:6], rest[6:]
    lat = lax.axis_size("lat")
    depth = lat // 4
    rows, width = embed.shape
    grid_rows, channels = state.shape
    vmem_spec = pl.BlockSpec(memory_space=pltpu.VMEM)
    hbm_spec = pl.BlockSpec(memory_space=pltpu.HBM)
    channel_pad = -(-channels // 128) * 128
    dma = pltpu.SemaphoreType.DMA
    gather_sems = [dma((4 * depth,)), dma((lat,))]
    result = pl.pallas_call(
        functools.partial(fused, depth),
        out_shape=jax.ShapeDtypeStruct((channels, grid_rows), BF16),
        in_specs=[vmem_spec] * 9 + [hbm_spec] * WEIGHTS,
        out_specs=vmem_spec,
        scratch_shapes=[pltpu.VMEM(w.shape, w.dtype) for w in weights[:WEIGHTS]]
        + [pltpu.VMEM((lat, rows, width), BF16)] * 4
        + [pltpu.VMEM((2, depth, rows, width), BF16)]
        + [pltpu.VMEM((depth, rows, width), BF16)] * 4
        + [pltpu.VMEM((grid_rows, width), F32)] * 2
        + [pltpu.VMEM((channel_pad, grid_rows), BF16), pltpu.VMEM((channel_pad, width), BF16)]
        + [dma((WEIGHTS,))]
        + gather_sems * 3
        + [dma((2,))] * 2
        + [dma((depth,))] * 4,
        compiler_params=pltpu.CompilerParams(
            collective_id=0, has_side_effects=True, vmem_limit_bytes=63 * 1024 * 1024
        ),
        cost_estimate=pl.CostEstimate(flops=2 * 10**9, bytes_accessed=10**7, transcendentals=10**6),
    )(state.T, embed, *[i.T for i in indices], weights[WEIGHTS].T, *weights[:WEIGHTS])
    return result.T


def solution(mesh):
    lat = mesh.shape["lat"]
    step = fused_body if lat % 4 == 0 and 8 <= lat <= 32 else body
    in_specs = (
        P(("groups", "lat"), None),
        P(("groups", "lat"), None),
        P(("groups", "lat"), None),
        P(("groups", "lat"), None),
        P(("groups", "lat"), None),
        P(("groups", "lat"), None),
        P(("groups", "lat"), None),
        P(("groups", "lat"), None),
        P(),
        P(),
        P(),
        P(),
        P(),
        P(),
        P(),
        P(),
        P(),
        P(),
        P(),
        P(),
        P(),
        P(),
    )
    out_specs = P(("groups", "lat"), None)
    return jax.shard_map(step, mesh=mesh, in_specs=in_specs, out_specs=out_specs, check_vma=False)
```
